32 devices in a mesh: comp: 2 (over x), lon: 8 (over z, core), ch: 2 (over y).
Axes of the slice: x: 2, y: 2, z: 4, core: 2. Of those that a mesh axis runs over, the one named last changes fastest.
Arguments:
- ocean_state: bfloat16 [3, 128, 64, 256], P(None, 'ch', ('comp', 'lon')), may hold values from -6 to 6
- ocean_mask: int32 [64, 256], P(('comp', 'lon')), may hold values 0 or 1
- air_state: bfloat16 [2, 192, 32, 2, 256], P(None, 'ch', 'lon', None, 'comp'), may hold values from -6 to 6
- surface_temp: float32 [64, 256], P(('comp', 'lon')), may hold values from -6 to 6
- air_fluxes: float32 [4, 32, 2, 256], P(None, 'lon', None, 'comp'), may hold values from -6 to 6
- ocean_kernel: float32 [128, 3, 7, 7], P('ch'), may hold values from -0.5 to 0.5
- ocean_gain: float32 [128], replicated, may hold values from 0.5 to 1.5
- ocean_up: bfloat16 [128, 512], replicated, may hold values from -0.5 to 0.5
- ocean_down: bfloat16 [512, 128], replicated, may hold values from -0.25 to 0.25
- air_kernel: float32 [192, 3, 7, 7], P('ch'), may hold values from -0.5 to 0.5
- air_gain: float32 [192], replicated, may hold values from 0.5 to 1.5
- air_up: bfloat16 [192, 768], replicated, may hold values from -0.4375 to 0.4375
- air_down: bfloat16 [768, 192], replicated, may hold values from -0.21875 to 0.21875
- flux_weight: float32 [4, 128], P(None, 'ch'), may hold values from -3 to 3
- temp_weight: float32 [192], P('ch'), may hold values from -1 to 1
Outputs:
- ocean_next: bfloat16 [3, 128, 64, 256], P(None, 'ch', ('comp', 'lon'))
- air_next: bfloat16 [2, 192, 32, 2, 256], P(None, 'ch', 'lon', None, 'comp')
The draws below stay inside these ranges and needn't reach their ends.
All inputs are finite; a program needn't handle non-finite values. No bound on the sum of `ocean_mask` on one device may be relied on, other than what follows from the above.
Results may differ from the reference program's by a relative error of at most 0.007.
Values may be sent and summed in bfloat16 or wider, within the bound.
A program may use at most 64 MiB of HBM per device.

```python
import jax
import jax.numpy as jnp
from jax import lax

OCEAN_LEV = 3
AIR_LEV = 2
OCEAN_CH = 128
OCEAN_HID = 512
AIR_CH = 192
AIR_HID = 768
NFLUX = 4
BAND = 4
NLAT = 256
NLON = 64
N_COMP = 2


def place_ends(array, key, least, high):
    index_at = [jax.random.randint(jax.random.fold_in(key, axis), (), 0, length) for axis, length in enumerate(array.shape)]
    longest = array.shape.index(max(array.shape))
    beside = index_at[:longest] + [(index_at[longest] + 1) % array.shape[longest]] + index_at[longest + 1:]
    return array.at[tuple(index_at)].set(least).at[tuple(beside)].set(high)


def steps_of(key, dims, cuts, low, top_value):
    level = 1.0
    for axis_at, blocks in cuts:
        heights = jax.random.uniform(jax.random.fold_in(jax.random.fold_in(key, 6), axis_at), (blocks,), jnp.float32, low / len(cuts), top_value / len(cuts))
        level = level * jnp.repeat(jnp.exp(heights), dims[axis_at] // blocks).reshape((-1,) + (1,) * (len(dims) - 1 - axis_at))
    return level


def centred(rng, dims, width, bound, pieces=(), kind=jnp.bfloat16):
    result = width * jax.random.normal(rng, dims, jnp.float32)
    if pieces:
        result = result * steps_of(rng, dims, pieces, -0.22, 0.18)
    return jnp.clip(result, -bound, bound).astype(kind)


def setup_inputs(seed: int = 0) -> dict:
    arg_keys = jax.random.split(jax.random.key(seed), 16)
    ocean_state = centred(arg_keys[0], (OCEAN_LEV, OCEAN_CH, NLON, NLAT), 1.0, 6.0, ((1, 2), (2, 16)))
    ocean_mask = place_ends((jax.random.randint(arg_keys[1], (NLON, NLAT), 0, 10) < 7).astype(jnp.int32), jax.random.fold_in(arg_keys[1], 1), 0, 1)
    air_state = centred(arg_keys[2], (AIR_LEV, AIR_CH, NLON // N_COMP, N_COMP, NLAT), 1.0, 6.0, ((1, 2), (2, 8), (4, 2)))
    surface_temp = centred(arg_keys[3], (NLON, NLAT), 1.0, 6.0, ((0, 16),), jnp.float32)
    air_fluxes = centred(arg_keys[4], (NFLUX, NLON // N_COMP, N_COMP, NLAT), 1.0, 6.0, ((1, 8), (3, 2)), jnp.float32)
    ocean_kernel = centred(arg_keys[5], (OCEAN_CH, 3, 7, 7), 147 ** -0.5, 0.5, ((0, 2),), jnp.float32)
    ocean_gain = jnp.clip(jax.random.uniform(arg_keys[6], (OCEAN_CH,), jnp.float32, 0.5, 1.5), 0.5, 1.5)
    ocean_up = centred(arg_keys[7], (OCEAN_CH, OCEAN_HID), OCEAN_CH ** -0.5, 0.5)
    ocean_down = centred(arg_keys[8], (OCEAN_HID, OCEAN_CH), OCEAN_HID ** -0.5, 0.25)
    air_kernel = centred(arg_keys[9], (AIR_CH, 3, 7, 7), 147 ** -0.5, 0.5, ((0, 2),), jnp.float32)
    air_gain = jnp.clip(jax.random.uniform(arg_keys[10], (AIR_CH,), jnp.float32, 0.5, 1.5), 0.5, 1.5)
    air_up = centred(arg_keys[11], (AIR_CH, AIR_HID), AIR_CH ** -0.5, 0.4375)
    air_down = centred(arg_keys[12], (AIR_HID, AIR_CH), AIR_HID ** -0.5, 0.21875)
    flux_weight = centred(arg_keys[13], (NFLUX, OCEAN_CH), NFLUX ** -0.5, 3.0, ((1, 2),), jnp.float32)
    temp_weight = jnp.clip(jax.random.uniform(arg_keys[14], (AIR_CH,), jnp.float32, -1.0, 1.0) * steps_of(arg_keys[14], (AIR_CH,), ((0, 2),), -0.4, 0.0), -1.0, 1.0)
    return {"ocean_state": ocean_state, "ocean_mask": ocean_mask, "air_state": air_state, "surface_temp": surface_temp, "air_fluxes": air_fluxes, "ocean_kernel": ocean_kernel, "ocean_gain": ocean_gain, "ocean_up": ocean_up, "ocean_down": ocean_down, "air_kernel": air_kernel, "air_gain": air_gain, "air_up": air_up, "air_down": air_down, "flux_weight": flux_weight, "temp_weight": temp_weight}


def periodic_conv(forced, kernel):
    channels = forced.shape[1]
    wrapped = jnp.concatenate([forced[:, :, -3:], forced, forced[:, :, :3]], axis=2)
    inputs = jnp.transpose(wrapped, (1, 0, 2, 3))[None]
    filters = kernel[:, None]
    output = lax.conv_general_dilated(inputs, filters, (1, 1, 1), ((1, 1), (0, 0), (3, 3)), dimension_numbers=('NCDHW', 'OIDHW', 'NCDHW'), feature_group_count=channels, precision=lax.Precision.HIGHEST)
    return jnp.transpose(output[0], (1, 0, 2, 3))

def channel_norm(conv_out, gain_vec):
    values = conv_out.astype(jnp.float32)
    center = lax.optimization_barrier(jnp.mean(values, axis=1, keepdims=True))
    spread = lax.optimization_barrier(jnp.mean(jnp.square(values - center), axis=1, keepdims=True))
    scaled = gain_vec.reshape((1, gain_vec.shape[0]) + (1,) * (values.ndim - 2))
    return ((values - center) * lax.rsqrt(spread + 1e-06) * scaled).astype(jnp.bfloat16)

def feed_forward(normed, up_proj, down_proj):
    hidden = jax.nn.gelu(jnp.einsum('ch,lcxy->lhxy', up_proj.astype(jnp.float32), normed.astype(jnp.float32), precision=lax.Precision.HIGHEST)).astype(jnp.bfloat16)
    return jnp.einsum('hc,lhxy->lcxy', down_proj.astype(jnp.float32), hidden.astype(jnp.float32), precision=lax.Precision.HIGHEST)

def block_update(conv_out, gain_vec, up_proj, down_proj):
    levels = conv_out.shape[0]
    channels = conv_out.shape[1]
    blocks = NLON // BAND
    tiled = jnp.transpose(conv_out.reshape(levels, channels, blocks, BAND, NLAT), (2, 0, 1, 3, 4))

    def one_block(piece):
        return feed_forward(channel_norm(piece, gain_vec), up_proj, down_proj).astype(jnp.bfloat16)
    updated = lax.map(one_block, tiled)
    return jnp.transpose(updated, (1, 2, 0, 3, 4)).reshape(levels, channels, NLON, NLAT)

def reference(ocean_state, ocean_mask, air_state, surface_temp, air_fluxes, ocean_kernel, ocean_gain, ocean_up, ocean_down, air_kernel, air_gain, air_up, air_down, flux_weight, temp_weight):
    sea_mask = ocean_mask.astype(jnp.float32)
    flux_grid = jnp.transpose(air_fluxes, (0, 2, 1, 3)).reshape(NFLUX, NLON, NLAT)
    inject = jnp.einsum('kc,kxy->cxy', flux_weight, flux_grid, precision=lax.Precision.HIGHEST)
    ocean_states = ocean_state.astype(jnp.float32)
    ocean_forced = jnp.concatenate([ocean_states[:1] + inject[None], ocean_states[1:]], axis=0) * sea_mask
    ocean_conv = periodic_conv(ocean_forced, ocean_kernel).astype(jnp.bfloat16)
    ocean_update = block_update(ocean_conv, ocean_gain, ocean_up, ocean_down)
    ocean_next = ((ocean_forced + ocean_update.astype(jnp.float32)) * sea_mask).astype(jnp.bfloat16)
    air_grid = jnp.transpose(air_state, (0, 1, 3, 2, 4)).reshape(AIR_LEV, AIR_CH, NLON, NLAT).astype(jnp.float32)
    heating = temp_weight[:, None, None] * (surface_temp * sea_mask)[None]
    air_forced = jnp.concatenate([air_grid[:1] + heating[None], air_grid[1:]], axis=0)
    air_conv = periodic_conv(air_forced, air_kernel).astype(jnp.bfloat16)
    air_update = block_update(air_conv, air_gain, air_up, air_down)
    air_final = (air_forced + air_update.astype(jnp.float32)).astype(jnp.bfloat16)
    air_next = jnp.transpose(air_final.reshape(AIR_LEV, AIR_CH, N_COMP, NLON // N_COMP, NLAT), (0, 1, 3, 2, 4))
    return (ocean_next, air_next)
```

```python
import functools

import jax
import jax.numpy as jnp
from jax import lax
from jax.experimental import pallas as pl
from jax.experimental.pallas import tpu as pltpu
from jax.sharding import PartitionSpec as P

LANES = 128
ROWS = 16
HALF = 8


def conv_taps(main, wrap, k_ref, rows, p, levels, width):
    lane = lax.broadcasted_iota(jnp.int32, (width + 6, HALF, LANES), 2)
    sums = [None] * levels
    for d in range(7):
        s = d - 3
        shifted = []
        for lev in range(levels):
            v = main[lev, p, :, rows, :]
            if s > 0:
                v = pltpu.roll(jnp.where(lane < s, wrap[lev, p], v), LANES - s, 2)
            elif s < 0:
                v = pltpu.roll(jnp.where(lane >= LANES + s, wrap[lev, p], v), -s, 2)
            shifted.append(v)
        for a in range(3):
            for b in range(7):
                tap = a * 49 + b * 7 + d
                w = jnp.broadcast_to(k_ref[rows, tap : tap + 1], (HALF, LANES))[None]
                for lev in range(levels):
                    src = lev + a - 1
                    if 0 <= src < levels:
                        term = w * shifted[src][b : b + width]
                        sums[lev] = term if sums[lev] is None else sums[lev] + term
    return sums


def ocean_conv_kernel(x_ref, k_ref, o_ref, main, wrap, total):
    levels, wide, _, lat = x_ref.shape
    tiles = lat // LANES
    width = wide - 6
    lane = lax.broadcasted_iota(jnp.int32, (wide, HALF, LANES), 2)
    for lev in range(levels):
        for p in range(tiles):
            main[lev, p] = x_ref[lev, :, :, p * LANES : (p + 1) * LANES].astype(jnp.float32)

    def body(sub, carry):
        rows = pl.ds(pl.multiple_of(sub * HALF, HALF), HALF)
        zero = jnp.zeros((wide, HALF, LANES), jnp.float32)
        for p in range(tiles):
            for lev in range(levels):
                high = main[lev, p + 1, :, rows, :] if p + 1 < tiles else zero
                low = main[lev, p - 1, :, rows, :] if p > 0 else zero
                wrap[lev, p] = jnp.where(lane < LANES // 2, high, low)
        for p in range(tiles):
            sums = conv_taps(main, wrap, k_ref, rows, p, levels, width)
            for lev in range(levels):
                total[lev, p, :, rows, :] = sums[lev]
        return carry

    lax.fori_loop(0, ROWS // HALF, body, 0)
    for lev in range(levels):
        for p in range(tiles):
            o_ref[lev, :, :, p * LANES : (p + 1) * LANES] = total[lev, p].astype(jnp.bfloat16)


def air_conv_kernel(x_ref, e_ref, k_ref, o_ref, main, wrap, total, edge):
    levels, halves, wide, _, _ = x_ref.shape
    width = wide - 6
    for lev in range(levels):
        edge[lev] = e_ref[lev].astype(jnp.float32)
        for p in range(halves):
            main[lev, p] = x_ref[lev, p].astype(jnp.float32)

    def body(sub, carry):
        rows = pl.ds(pl.multiple_of(sub * HALF, HALF), HALF)
        for lev in range(levels):
            e = edge[lev, rows, :]
            for p in range(halves):
                for m in range(wide):
                    base = (p * wide + m) * 6 + 3
                    wrap[lev, p, m] = pltpu.roll(e, LANES - base, 1)
        for p in range(halves):
            sums = conv_taps(main, wrap, k_ref, rows, p, levels, width)
            for lev in range(levels):
                total[lev, p, :, rows, :] = sums[lev]
        return carry

    lax.fori_loop(0, ROWS // HALF, body, 0)
    for lev in range(levels):
        for p in range(halves):
            o_ref[lev, p] = total[lev, p].astype(jnp.bfloat16)


def conv_scratch(levels, tiles, wide):
    return [
        pltpu.VMEM((levels, tiles, wide, ROWS, LANES), jnp.float32),
        pltpu.VMEM((levels, tiles, wide, HALF, LANES), jnp.float32),
        pltpu.VMEM((levels, tiles, wide - 6, ROWS, LANES), jnp.float32),
    ]


def ocean_conv(x, k):
    levels, wide, ch, lat = x.shape
    return pl.pallas_call(
        ocean_conv_kernel,
        grid=(ch // ROWS,),
        in_specs=[
            pl.BlockSpec((levels, wide, ROWS, lat), lambda g: (0, 0, g, 0)),
            pl.BlockSpec((ROWS, k.shape[1]), lambda g: (g, 0)),
        ],
        out_specs=pl.BlockSpec((levels, wide - 6, ROWS, lat), lambda g: (0, 0, g, 0)),
        out_shape=jax.ShapeDtypeStruct((levels, wide - 6, ch, lat), jnp.bfloat16),
        scratch_shapes=conv_scratch(levels, lat // LANES, wide),
        compiler_params=pltpu.CompilerParams(vmem_limit_bytes=32 * 1024 * 1024),
        cost_estimate=pl.CostEstimate(
            flops=25_000_000, bytes_accessed=1_500_000, transcendentals=0
        ),
    )(x, k)


def air_conv(x, e, k):
    levels, halves, wide, ch, lat = x.shape
    return pl.pallas_call(
        air_conv_kernel,
        grid=(ch // ROWS,),
        in_specs=[
            pl.BlockSpec((levels, halves, wide, ROWS, lat), lambda g: (0, 0, 0, g, 0)),
            pl.BlockSpec((levels, ROWS, LANES), lambda g: (0, g, 0)),
            pl.BlockSpec((ROWS, k.shape[1]), lambda g: (g, 0)),
        ],
        out_specs=pl.BlockSpec((levels, halves, wide - 6, ROWS, lat), lambda g: (0, 0, 0, g, 0)),
        out_shape=jax.ShapeDtypeStruct((levels, halves, wide - 6, ch, lat), jnp.bfloat16),
        scratch_shapes=conv_scratch(levels, halves, wide)
        + [pltpu.VMEM((levels, ROWS, LANES), jnp.float32)],
        compiler_params=pltpu.CompilerParams(vmem_limit_bytes=32 * 1024 * 1024),
        cost_estimate=pl.CostEstimate(
            flops=20_000_000, bytes_accessed=1_500_000, transcendentals=0
        ),
    )(x, e, k)


def mlp_kernel(mine_ref, other_ref, res_ref, gain_ref, up_ref, down_ref, sea_ref, o_ref):
    count = mine_ref.shape[1]

    def wide(ref):
        return jnp.concatenate([ref[0, i] for i in range(count)], axis=1)

    values = jnp.concatenate([wide(mine_ref), wide(other_ref)], axis=0).astype(jnp.float32)
    center = jnp.mean(values, axis=0, keepdims=True)
    moved = values - center
    spread = jnp.mean(moved * moved, axis=0, keepdims=True)
    normed = (moved * lax.rsqrt(spread + 1e-06) * gain_ref[...]).astype(jnp.bfloat16)
    raw = jnp.dot(up_ref[...], normed, preferred_element_type=jnp.float32)
    hidden = jax.nn.gelu(raw).astype(jnp.bfloat16)
    update = jnp.dot(down_ref[...], hidden, preferred_element_type=jnp.float32)
    update = update.astype(jnp.bfloat16).astype(jnp.float32)
    out = wide(res_ref).astype(jnp.float32) + update
    lat = mine_ref.shape[3]
    for i in range(count):
        piece = out[:, i * lat : (i + 1) * lat]
        if sea_ref is not None:
            piece = piece * sea_ref[i : i + 1, :].astype(jnp.float32)
        o_ref[0, i] = piece.astype(jnp.bfloat16)


def mlp(mine, other, resid, gain, up, down, sea, count):
    lead, cols, ch, lat = mine.shape
    block = pl.BlockSpec((1, count, ch, lat), lambda i, j: (i, j, 0, 0))
    whole = lambda arr: pl.BlockSpec(arr.shape, lambda i, j: (0,) * arr.ndim)
    ins = [mine, other, resid, gain, up, down]
    specs = [block, block, block, whole(gain), whole(up), whole(down)]
    kernel = mlp_kernel
    if sea is None:
        kernel = lambda m, t, r, g, u, d, o: mlp_kernel(m, t, r, g, u, d, None, o)
    else:
        ins.append(sea)
        specs.append(whole(sea))
    return pl.pallas_call(
        kernel,
        grid=(lead, cols // count),
        in_specs=specs,
        out_specs=block,
        out_shape=jax.ShapeDtypeStruct(mine.shape, jnp.bfloat16),
        compiler_params=pltpu.CompilerParams(vmem_limit_bytes=32 * 1024 * 1024),
        cost_estimate=pl.CostEstimate(
            flops=600_000_000, bytes_accessed=2_000_000, transcendentals=1_500_000
        ),
    )(*ins)


def ring(axis):
    count = lax.axis_size(axis)
    forward = [(i, (i + 1) % count) for i in range(count)]
    return forward, [(t, s) for s, t in forward]


def per_device(
    ocean_state,
    ocean_mask,
    air_state,
    surface_temp,
    air_fluxes,
    ocean_kernel,
    ocean_gain,
    ocean_up,
    ocean_down,
    air_kernel,
    air_gain,
    air_up,
    air_down,
    flux_weight,
    temp_weight,
):
    f32, bf16 = jnp.float32, jnp.bfloat16
    comp = lax.axis_index("comp")
    lon = lax.axis_index("lon")
    bands = lax.axis_size("lon")
    swap = [(0, 1), (1, 0)]
    first = comp == 0
    band = ocean_state.shape[2]
    lat = ocean_state.shape[3]
    part = air_state.shape[4]
    air_lev, air_ch = air_state.shape[:2]

    sea = ocean_mask.astype(f32)
    own_temp = surface_temp * sea
    own_flux = jnp.where(first, air_fluxes[:, :, 0], air_fluxes[:, :, 1])
    sent_flux = jnp.where(first, air_fluxes[:, :, 1], air_fluxes[:, :, 0])
    sent_edge = jnp.where(first, air_state[..., -3:], air_state[..., :3])
    sent_edge = jnp.transpose(sent_edge, (0, 1, 3, 2, 4)).reshape(air_lev, air_ch, -1)
    got_temp = lax.ppermute(own_temp, "comp", swap)
    got_flux = lax.ppermute(sent_flux, "comp", swap)
    got_edge = lax.ppermute(sent_edge, "comp", swap)

    flux = jnp.where(
        first,
        jnp.concatenate([own_flux, got_flux], axis=-1),
        jnp.concatenate([got_flux, own_flux], axis=-1),
    )
    state = jnp.transpose(ocean_state, (0, 2, 1, 3)).astype(f32)
    inject = sum(
        flux_weight[k][None, :, None] * flux[k][:, None, :] for k in range(flux.shape[0])
    )
    forced = jnp.concatenate([state[:1] + inject[None], state[1:]], axis=0)
    forced = (forced * sea[None, :, None, :]).astype(bf16)
    forward, backward = ring(("comp", "lon"))
    west = lax.ppermute(forced[:, -3:], ("comp", "lon"), forward)
    east = lax.ppermute(forced[:, :3], ("comp", "lon"), backward)

    temp = jnp.where(first, jnp.stack([own_temp, got_temp]), jnp.stack([got_temp, own_temp]))
    temp = jnp.pad(temp, ((0, 0), (0, 0), (3, 3)))
    temp = lax.dynamic_slice_in_dim(temp, comp * part, part + 6, 2)
    air = jnp.transpose(air_state, (0, 3, 2, 1, 4)).astype(f32)
    heat = temp_weight[None, None, :, None] * temp[:, :, None, 3 : 3 + part]
    air = jnp.concatenate([air[:1] + heat[None], air[1:]], axis=0).astype(bf16)
    got_edge = got_edge.reshape(air_lev, air_ch, 2, band, 3).astype(f32)
    zero = jnp.zeros_like(got_edge)
    edge = jnp.where(
        first,
        jnp.concatenate([zero, got_edge], axis=-1),
        jnp.concatenate([got_edge, zero], axis=-1),
    )
    rim = jnp.concatenate([temp[:, :, :3], temp[:, :, -3:]], axis=-1)
    rim = temp_weight[:, None, None, None] * rim[None]
    edge = jnp.concatenate([edge[:1] + rim[None], edge[1:]], axis=0).astype(bf16)
    forward, backward = ring("lon")
    air_west = lax.ppermute(air[:, :, -3:], "lon", forward)
    air_east = lax.ppermute(air[:, :, :3], "lon", backward)
    edge_shape = (air_lev, air_ch, -1)
    edge_west = lax.ppermute(edge[:, :, :, -3:].reshape(edge_shape), "lon", forward)
    edge_east = lax.ppermute(edge[:, :, :, :3].reshape(edge_shape), "lon", backward)
    halo_shape = (air_lev, air_ch, 2, 3, 6)
    edge_west = edge_west.reshape(halo_shape)
    edge_east = edge_east.reshape(halo_shape)
    at_west, at_east = lon == 0, lon == bands - 1
    air_west = jnp.where(at_west, air_west[:, ::-1], air_west)
    air_east = jnp.where(at_east, air_east[:, ::-1], air_east)
    edge_west = jnp.where(at_west, edge_west[:, :, ::-1], edge_west)
    edge_east = jnp.where(at_east, edge_east[:, :, ::-1], edge_east)

    forced_wide = jnp.concatenate([west, forced, east], axis=1)
    ocean_mine = ocean_conv(forced_wide, ocean_kernel.reshape(ocean_kernel.shape[0], -1))
    ocean_other = lax.ppermute(ocean_mine, "ch", swap)
    air_wide = jnp.concatenate([air_west, air, air_east], axis=2)
    edges = jnp.concatenate([edge_west, edge, edge_east], axis=3).reshape(edge_shape)
    edges = jnp.pad(edges, ((0, 0), (0, 0), (0, LANES - edges.shape[-1])))
    air_mine = air_conv(air_wide, edges, air_kernel.reshape(air_kernel.shape[0], -1))
    air_other = lax.ppermute(air_mine, "ch", swap)

    at = lax.axis_index("ch")

    def mine_first(array, axis):
        low, high = jnp.split(array, 2, axis=axis)
        return jnp.where(
            at == 0,
            jnp.concatenate([low, high], axis=axis),
            jnp.concatenate([high, low], axis=axis),
        )

    def mine_only(array):
        low, high = jnp.split(array, 2, axis=1)
        return jnp.where(at == 0, low, high).T

    ocean_next = mlp(
        ocean_mine,
        ocean_other,
        forced,
        mine_first(ocean_gain, 0)[:, None],
        mine_first(ocean_up, 0).T,
        mine_only(ocean_down),
        ocean_mask,
        band,
    )
    flat = lambda v: v.reshape((air_lev * 2,) + v.shape[2:])
    air_next = mlp(
        flat(air_mine),
        flat(air_other),
        flat(air),
        mine_first(air_gain, 0)[:, None],
        mine_first(air_up, 0).T,
        mine_only(air_down),
        None,
        band,
    )
    air_next = air_next.reshape(air.shape)
    return jnp.transpose(ocean_next, (0, 2, 1, 3)), jnp.transpose(air_next, (0, 3, 2, 1, 4))


def solution(mesh):
    in_specs = (
        P(None, "ch", ("comp", "lon"), None),
        P(("comp", "lon"), None),
        P(None, "ch", "lon", None, "comp"),
        P(("comp", "lon"), None),
        P(None, "lon", None, "comp"),
        P("ch", None, None, None),
        P(),
        P(),
        P(),
        P("ch", None, None, None),
        P(),
        P(),
        P(),
        P(None, "ch"),
        P("ch"),
    )
    out_specs = (P(None, "ch", ("comp", "lon"), None), P(None, "ch", "lon", None, "comp"))
    return jax.shard_map(
        per_device, mesh=mesh, in_specs=in_specs, out_specs=out_specs, check_vma=False
    )
```

```python
import functools

import jax
import jax.numpy as jnp
from jax import lax
from jax.experimental import pallas as pl
from jax.experimental.pallas import tpu as pltpu
from jax.sharding import PartitionSpec as P

LANES = 128
ROWS = 16
HALF = 8
RIM = 3
TAPS = 147
MESH = pl.DeviceIdType.MESH
F32, BF16 = jnp.float32, jnp.bfloat16


def tap_sum(values, wb, group, d, levels, width):
    sums = [None] * levels
    for a in range(3):
        for b in range(7):
            w = wb[group, a * 49 + b * 7 + d][None]
            for lev in range(levels):
                src = lev + a - 1
                if 0 <= src < levels:
                    term = w * values(src, b)
                    sums[lev] = term if sums[lev] is None else sums[lev] + term
    return sums


def ocean_group(main, wb, total, rows, group, levels, tiles, width):
    lane = lax.broadcasted_iota(jnp.int32, (width, HALF, LANES), 2)
    zero = jnp.zeros((width, HALF, LANES), F32)
    for step, d in enumerate((3, 0, 1, 2, 4, 5, 6)):
        s = d - 3
        sums = [
            tap_sum(lambda lev, b: main[lev, p, b : b + width, rows, :], wb, group, d, levels, width)
            for p in range(tiles)
        ]
        for p in range(tiles):
            for lev in range(levels):
                v = sums[p][lev]
                if s > 0:
                    beside = sums[p + 1][lev] if p + 1 < tiles else zero
                    v = pltpu.roll(jnp.where(lane < s, beside, v), LANES - s, 2)
                elif s < 0:
                    beside = sums[p - 1][lev] if p > 0 else zero
                    v = pltpu.roll(jnp.where(lane >= LANES + s, beside, v), -s, 2)
                if step == 0:
                    total[lev, p, :, rows, :] = v
                else:
                    total[lev, p, :, rows, :] += v


def air_group(main, wrap, wb, total, rows, group, levels, halves, width):
    lane = lax.broadcasted_iota(jnp.int32, (width + 2 * RIM, HALF, LANES), 2)
    for p in range(halves):
        for step, d in enumerate((3, 0, 1, 2, 4, 5, 6)):
            s = d - 3
            shifted = []
            for lev in range(levels):
                v = main[lev, p, :, rows, :]
                if s > 0:
                    v = pltpu.roll(jnp.where(lane < s, wrap[lev, p], v), LANES - s, 2)
                elif s < 0:
                    v = pltpu.roll(jnp.where(lane >= LANES + s, wrap[lev, p], v), -s, 2)
                shifted.append(v)
            sums = tap_sum(lambda lev, b: shifted[lev][b : b + width], wb, group, d, levels, width)
            for lev in range(levels):
                if step == 0:
                    total[lev, p, :, rows, :] = sums[lev]
                else:
                    total[lev, p, :, rows, :] += sums[lev]


def spread_taps(k_ref, wb):
    def body(group, carry):
        rows = pl.ds(pl.multiple_of(group * HALF, HALF), HALF)
        taps = k_ref[rows, :]
        for tap in range(TAPS):
            wb[group, tap] = jnp.broadcast_to(taps[:, tap : tap + 1], (HALF, LANES))
        return carry

    lax.fori_loop(0, wb.shape[0], body, 0)


def mlp(mine, other, resid, gain, up, down):
    values = jnp.concatenate([mine, other], axis=0).astype(F32)
    center = jnp.mean(values, axis=0, keepdims=True)
    moved = values - center
    spread = jnp.mean(moved * moved, axis=0, keepdims=True)
    normed = (moved * lax.rsqrt(spread + 1e-06) * gain).astype(BF16)
    hidden = jax.nn.gelu(jnp.dot(up, normed, preferred_element_type=F32)).astype(BF16)
    update = jnp.dot(down, hidden, preferred_element_type=F32)
    return resid.astype(F32) + update.astype(BF16).astype(F32)


def step_kernel(
    bands,
    state_ref,
    mask_ref,
    air_ref,
    temp_ref,
    flux_ref,
    ok_ref,
    ak_ref,
    cols_ref,
    oup_ref,
    odown_ref,
    aup_ref,
    adown_ref,
    onext_ref,
    anext_ref,
    tl,
    fs,
    fl,
    es,
    er,
    ec,
    ew,
    ee,
    edge,
    ow,
    aw,
    oc,
    oo,
    ac,
    ao,
    owb,
    awb,
    omain,
    ototal,
    amain,
    awrap,
    atotal,
    send,
    recv,
    osend,
    orecv,
    asend,
    arecv,
):
    levels, band, och, lat = state_ref.shape
    alevels, halves, _, ach, part = air_ref.shape
    tiles = lat // LANES
    wide = band + 2 * RIM
    span = wide * 2 * RIM
    fields = fs.shape[0]
    last = band + RIM
    comp = lax.axis_index("comp")
    lon = lax.axis_index("lon")
    at = lax.axis_index("ch")
    count = 2 * bands
    place = comp * bands + lon
    west = lax.rem(place + count - 1, count)
    east = lax.rem(place + 1, count)
    o_west = {"comp": lax.div(west, bands), "lon": lax.rem(west, bands)}
    o_east = {"comp": lax.div(east, bands), "lon": lax.rem(east, bands)}
    a_west = {"lon": lax.rem(lon + bands - 1, bands)}
    a_east = {"lon": lax.rem(lon + 1, bands)}
    over = {"comp": 1 - comp}
    pair = {"ch": 1 - at}
    at_west = (lon == 0).astype(jnp.int32)
    at_east = (lon == bands - 1).astype(jnp.int32)

    barrier = pltpu.get_barrier_semaphore()
    for device in (over, pair, o_west, o_east, a_west, a_east):
        pl.semaphore_signal(barrier, inc=1, device_id=device, device_id_type=MESH)

    started = []

    def copy(src, dst, device):
        i = len(started)
        made = pltpu.make_async_remote_copy(
            src_ref=src,
            dst_ref=dst,
            send_sem=send.at[i],
            recv_sem=recv.at[i],
            device_id=device,
            device_id_type=MESH,
        )
        made.start()
        started.append(made)
        return made

    sea = mask_ref[...].astype(F32)
    own_temp = temp_ref[...] * sea
    for p in range(2):
        tl[comp, p] = own_temp[:, p * part : (p + 1) * part]
    for k in range(fields):
        low, high = flux_ref[k, :, 0, :], flux_ref[k, :, 1, :]
        fs[k] = jnp.where(comp == 0, high, low)
        fl[comp, k] = jnp.where(comp == 0, low, high)
    lane = lax.broadcasted_iota(jnp.int32, (ach, LANES), 1)

    def pack(tile, into, h, j, owner):
        base = (h * wide + RIM + j) * 2 * RIM
        begin = base + RIM * owner
        here = (lane >= begin) & (lane < begin + RIM)
        return jnp.where(here, pltpu.roll(tile, base + RIM, 1), into)

    for lev in range(alevels):
        packed = jnp.zeros((ach, LANES), F32)
        for h in range(halves):
            for j in range(band):
                packed = pack(air_ref[lev, h, j].astype(F32), packed, h, j, comp)
        es[lev] = packed.astype(BF16)
    for lev in range(1, levels):
        for j in range(band):
            v = state_ref[lev, j].astype(F32) * sea[j : j + 1, :]
            ow[lev, RIM + j] = v.astype(BF16)

    pl.semaphore_wait(barrier, 6)
    got_temp = copy(tl.at[comp], tl.at[comp], over)
    got_flux = copy(fs, fl.at[comp], over)
    got_edge = copy(es, er, over)
    deep = pl.ds(1, levels - 1)
    top = pl.ds(0, 1)
    first, final = pl.ds(RIM, RIM), pl.ds(last - RIM, RIM)
    low_rim, high_rim = pl.ds(0, RIM), pl.ds(last, RIM)
    ocean_rims = [
        copy(ow.at[deep, first], ow.at[deep, high_rim], o_west),
        copy(ow.at[deep, final], ow.at[deep, low_rim], o_east),
    ]

    got_flux.wait_recv()
    for j in range(band):
        for p in range(tiles):
            inject = jnp.zeros((och, LANES), F32)
            for k in range(fields):
                inject += cols_ref[0:och, 3 + k : 4 + k] * fl[p, k, j : j + 1, :]
            cells = slice(p * LANES, (p + 1) * LANES)
            v = (state_ref[0, j, :, cells].astype(F32) + inject) * sea[j : j + 1, cells]
            ow[0, RIM + j, :, cells] = v.astype(BF16)
    ocean_rims.append(copy(ow.at[top, first], ow.at[top, high_rim], o_west))
    ocean_rims.append(copy(ow.at[top, final], ow.at[top, low_rim], o_east))

    got_temp.wait_recv()
    weight = cols_ref[0:ach, 2:3]
    for h in range(halves):
        for j in range(band):
            heat = weight * tl[h, comp, j : j + 1, :]
            aw[0, h, RIM + j] = (air_ref[0, h, j].astype(F32) + heat).astype(BF16)
            for lev in range(1, alevels):
                aw[lev, h, RIM + j] = air_ref[lev, h, j]
    air_rims = []
    every = pl.ds(0, alevels)
    for h in range(halves):
        to_west = lax.rem(h + (halves - 1) * at_west, halves)
        to_east = lax.rem(h + at_east, halves)
        air_rims.append(copy(aw.at[every, h, first], aw.at[every, to_west, high_rim], a_west))
        air_rims.append(copy(aw.at[every, h, final], aw.at[every, to_east, low_rim], a_east))
    got_edge.wait_recv()
    beyond = jnp.zeros((ach, LANES), F32)
    for h in range(halves):
        for j in range(band):
            row = jnp.broadcast_to(tl[h, 1 - comp, j : j + 1, :], (ach, LANES))
            beyond = pack(row, beyond, h, j, 1 - comp)
    ec[0] = (er[0].astype(F32) + weight * beyond).astype(BF16)
    for lev in range(1, alevels):
        ec[lev] = er[lev]
    edge_rims = [copy(ec, ee, a_west), copy(ec, ew, a_east)]

    spread_taps(ok_ref, owb)
    spread_taps(ak_ref, awb)

    for made in ocean_rims:
        made.wait_recv()

    def ocean_copy(g):
        rows = pl.ds(pl.multiple_of(g * ROWS, ROWS), ROWS)
        return pltpu.make_async_remote_copy(
            src_ref=oc.at[:, :, rows, :],
            dst_ref=oo.at[:, :, rows, :],
            send_sem=osend.at[g],
            recv_sem=orecv.at[g],
            device_id=pair,
            device_id_type=MESH,
        )

    def ocean_body(g, carry):
        wider = pl.ds(pl.multiple_of(g * ROWS, ROWS), ROWS)
        for lev in range(levels):
            for p in range(tiles):
                cells = slice(p * LANES, (p + 1) * LANES)
                omain[lev, p] = ow[lev, :, wider, cells].astype(F32)

        def inner(sub, carry):
            rows = pl.ds(pl.multiple_of(sub * HALF, HALF), HALF)
            group = g * (ROWS // HALF) + sub
            ocean_group(omain, owb, ototal, rows, group, levels, tiles, band)
            return carry

        lax.fori_loop(0, ROWS // HALF, inner, 0)
        for lev in range(levels):
            for p in range(tiles):
                cells = slice(p * LANES, (p + 1) * LANES)
                oc[lev, :, wider, cells] = ototal[lev, p].astype(BF16)
        ocean_copy(g).start()
        return carry

    lax.fori_loop(0, och // ROWS, ocean_body, 0)

    for made in air_rims + edge_rims:
        made.wait_recv()
    step = band * 2 * RIM
    for lev in range(alevels):
        from_west, from_east = ew[lev].astype(F32), ee[lev].astype(F32)
        whole = ec[lev].astype(F32)
        for h in range(halves):
            west_h = lax.rem(h + (halves - 1) * at_west, halves)
            east_h = lax.rem(h + at_east, halves)
            shift = lax.rem((h - west_h) * span - step + 2 * LANES, LANES)
            here = (lane >= h * span) & (lane < h * span + 2 * RIM * RIM)
            whole = jnp.where(here, pltpu.roll(from_west, shift, 1), whole)
            shift = lax.rem((h - east_h) * span + step + 2 * LANES, LANES)
            here = (lane >= (h + 1) * span - 2 * RIM * RIM) & (lane < (h + 1) * span)
            whole = jnp.where(here, pltpu.roll(from_east, shift, 1), whole)
        edge[lev] = whole

    def air_copy(g):
        rows = pl.ds(pl.multiple_of(g * ROWS, ROWS), ROWS)
        return pltpu.make_async_remote_copy(
            src_ref=ac.at[:, :, :, rows, :],
            dst_ref=ao.at[:, :, :, rows, :],
            send_sem=asend.at[g],
            recv_sem=arecv.at[g],
            device_id=pair,
            device_id_type=MESH,
        )

    def air_body(g, carry):
        wider = pl.ds(pl.multiple_of(g * ROWS, ROWS), ROWS)
        for lev in range(alevels):
            for p in range(halves):
                amain[lev, p] = aw[lev, p, :, wider, :].astype(F32)

        def inner(sub, carry):
            rows = pl.ds(pl.multiple_of(sub * HALF, HALF), HALF)
            group = g * (ROWS // HALF) + sub
            these = pl.ds(pl.multiple_of(group * HALF, HALF), HALF)
            for lev in range(alevels):
                e = edge[lev, these, :]
                for p in range(halves):
                    for m in range(wide):
                        awrap[lev, p, m] = pltpu.roll(e, LANES - (p * wide + m) * 2 * RIM - RIM, 1)
            air_group(amain, awrap, awb, atotal, rows, group, alevels, halves, band)
            return carry

        lax.fori_loop(0, ROWS // HALF, inner, 0)
        for lev in range(alevels):
            for p in range(halves):
                ac[lev, p, :, wider, :] = atotal[lev, p].astype(BF16)
        air_copy(g).start()
        return carry

    lax.fori_loop(0, ach // ROWS, air_body, 0)

    def flat(cells):
        return jnp.concatenate([cells[j] for j in range(band)], axis=1)

    def ordered(column, ch):
        mine = cols_ref[pl.ds(pl.multiple_of(at * ch, HALF), ch), column : column + 1]
        other = cols_ref[pl.ds(pl.multiple_of((1 - at) * ch, HALF), ch), column : column + 1]
        return jnp.concatenate([mine, other], axis=0)

    lax.fori_loop(0, och // ROWS, lambda g, c: (ocean_copy(g).wait(), c)[1], 0)
    gain = ordered(0, och)

    def ocean_mlp(lev, carry):
        resid = flat(ow[lev, RIM : RIM + band])
        out = mlp(flat(oc[lev]), flat(oo[lev]), resid, gain, oup_ref[...], odown_ref[...])
        for j in range(band):
            v = out[:, j * lat : (j + 1) * lat] * mask_ref[j : j + 1, :].astype(F32)
            onext_ref[lev, j] = v.astype(BF16)
        return carry

    lax.fori_loop(0, levels, ocean_mlp, 0)
    lax.fori_loop(0, ach // ROWS, lambda g, c: (air_copy(g).wait(), c)[1], 0)
    again = ordered(1, ach)

    def air_mlp(i, carry):
        lev, h = lax.div(i, halves), lax.rem(i, halves)
        resid = flat(aw[lev, h, RIM : RIM + band])
        out = mlp(flat(ac[lev, h]), flat(ao[lev, h]), resid, again, aup_ref[...], adown_ref[...])
        for j in range(band):
            anext_ref[lev, h, j] = out[:, j * part : (j + 1) * part].astype(BF16)
        return carry

    lax.fori_loop(0, alevels * halves, air_mlp, 0)
    for made in started:
        made.wait_send()


def per_device(
    ocean_state,
    ocean_mask,
    air_state,
    surface_temp,
    air_fluxes,
    ocean_kernel,
    ocean_gain,
    ocean_up,
    ocean_down,
    air_kernel,
    air_gain,
    air_up,
    air_down,
    flux_weight,
    temp_weight,
):
    bands = lax.axis_size("lon")
    at = lax.axis_index("ch")
    state = jnp.transpose(ocean_state, (0, 2, 1, 3))
    air = jnp.transpose(air_state, (0, 3, 2, 1, 4))
    levels, band, och, lat = state.shape
    alevels, halves, _, ach, part = air.shape
    fields = air_fluxes.shape[0]
    wide = band + 2 * RIM
    tiles = lat // LANES
    height = max(ocean_gain.shape[0], air_gain.shape[0])
    column = lambda v: jnp.pad(v, ((0, height - v.shape[0]), (0, 0)))
    cols = jnp.concatenate(
        [
            column(ocean_gain[:, None]),
            column(air_gain[:, None]),
            column(temp_weight[:, None]),
            column(flux_weight.T),
        ],
        axis=1,
    )

    def mine_first(array):
        low, high = jnp.split(array, 2, axis=0)
        return jnp.where(at == 0, array, jnp.concatenate([high, low], axis=0)).T

    def mine_only(array):
        low, high = jnp.split(array, 2, axis=1)
        return jnp.where(at == 0, low, high).T

    edge = (alevels, ach, LANES)
    scratch = [
        pltpu.VMEM((halves, 2, band, part), F32),
        pltpu.VMEM((fields, band, part), F32),
        pltpu.VMEM((2, fields, band, part), F32),
        pltpu.VMEM(edge, BF16),
        pltpu.VMEM(edge, BF16),
        pltpu.VMEM(edge, BF16),
        pltpu.VMEM(edge, BF16),
        pltpu.VMEM(edge, BF16),
        pltpu.VMEM(edge, F32),
        pltpu.VMEM((levels, wide, och, lat), BF16),
        pltpu.VMEM((alevels, halves, wide, ach, part), BF16),
        pltpu.VMEM(state.shape, BF16),
        pltpu.VMEM(state.shape, BF16),
        pltpu.VMEM(air.shape, BF16),
        pltpu.VMEM(air.shape, BF16),
        pltpu.VMEM((och // HALF, TAPS, HALF, LANES), F32),
        pltpu.VMEM((ach // HALF, TAPS, HALF, LANES), F32),
        pltpu.VMEM((levels, tiles, wide, ROWS, LANES), F32),
        pltpu.VMEM((levels, tiles, band, ROWS, LANES), F32),
        pltpu.VMEM((alevels, halves, wide, ROWS, LANES), F32),
        pltpu.VMEM((alevels, halves, wide, HALF, LANES), F32),
        pltpu.VMEM((alevels, halves, band, ROWS, LANES), F32),
        pltpu.SemaphoreType.DMA((9 + 2 * halves,)),
        pltpu.SemaphoreType.DMA((9 + 2 * halves,)),
        pltpu.SemaphoreType.DMA((och // ROWS,)),
        pltpu.SemaphoreType.DMA((och // ROWS,)),
        pltpu.SemaphoreType.DMA((ach // ROWS,)),
        pltpu.SemaphoreType.DMA((ach // ROWS,)),
    ]
    vmem = pl.BlockSpec(memory_space=pltpu.VMEM)
    ocean_next, air_next = pl.pallas_call(
        functools.partial(step_kernel, bands),
        out_shape=(
            jax.ShapeDtypeStruct(state.shape, BF16),
            jax.ShapeDtypeStruct(air.shape, BF16),
        ),
        in_specs=[vmem] * 12,
        out_specs=(vmem, vmem),
        scratch_shapes=scratch,
        compiler_params=pltpu.CompilerParams(
            collective_id=0, has_side_effects=True, vmem_limit_bytes=52 * 1024 * 1024
        ),
        cost_estimate=pl.CostEstimate(
            flops=2_000_000_000, bytes_accessed=4_000_000, transcendentals=3_000_000
        ),
    )(
        state,
        ocean_mask,
        air,
        surface_temp,
        air_fluxes,
        ocean_kernel.reshape(och, -1),
        air_kernel.reshape(ach, -1),
        cols,
        mine_first(ocean_up),
        mine_only(ocean_down),
        mine_first(air_up),
        mine_only(air_down),
    )
    return jnp.transpose(ocean_next, (0, 2, 1, 3)), jnp.transpose(air_next, (0, 3, 2, 1, 4))


def solution(mesh):
    in_specs = (
        P(None, "ch", ("comp", "lon"), None),
        P(("comp", "lon"), None),
        P(None, "ch", "lon", None, "comp"),
        P(("comp", "lon"), None),
        P(None, "lon", None, "comp"),
        P("ch", None, None, None),
        P(),
        P(),
        P(),
        P("ch", None, None, None),
        P(),
        P(),
        P(),
        P(None, "ch"),
        P("ch"),
    )
    out_specs = (P(None, "ch", ("comp", "lon"), None), P(None, "ch", "lon", None, "comp"))
    return jax.shard_map(
        per_device, mesh=mesh, in_specs=in_specs, out_specs=out_specs, check_vma=False
    )
```

```python
import functools

import jax
import jax.numpy as jnp
from jax import lax
from jax.experimental import pallas as pl
from jax.experimental.pallas import tpu as pltpu
from jax.sharding import PartitionSpec as P

LANES = 128
ROWS = 16
HALF = 8
RIM = 3
TAPS = 147
MESH = pl.DeviceIdType.MESH
F32, BF16 = jnp.float32, jnp.bfloat16


def tap_sum(values, wb, group, d, levels, width):
    sums = [None] * levels
    for a in range(3):
        for b in range(7):
            w = wb[group, a * 49 + b * 7 + d][None]
            for lev in range(levels):
                src = lev + a - 1
                if 0 <= src < levels:
                    term = w * values(src, b)
                    sums[lev] = term if sums[lev] is None else sums[lev] + term
    return sums


def ocean_group(main, wb, total, rows, group, levels, tiles, width):
    lane = lax.broadcasted_iota(jnp.int32, (width, HALF, LANES), 2)
    zero = jnp.zeros((width, HALF, LANES), F32)
    for step, d in enumerate((3, 0, 1, 2, 4, 5, 6)):
        s = d - 3
        sums = [
            tap_sum(lambda lev, b: main[lev, p, b : b + width, rows, :], wb, group, d, levels, width)
            for p in range(tiles)
        ]
        for p in range(tiles):
            for lev in range(levels):
                v = sums[p][lev]
                if s > 0:
                    beside = sums[p + 1][lev] if p + 1 < tiles else zero
                    v = pltpu.roll(jnp.where(lane < s, beside, v), LANES - s, 2)
                elif s < 0:
                    beside = sums[p - 1][lev] if p > 0 else zero
                    v = pltpu.roll(jnp.where(lane >= LANES + s, beside, v), -s, 2)
                if step == 0:
                    total[lev, p, :, rows, :] = v
                else:
                    total[lev, p, :, rows, :] += v


def air_group(main, wrap, wb, total, rows, group, levels, halves, width):
    lane = lax.broadcasted_iota(jnp.int32, (width + 2 * RIM, HALF, LANES), 2)
    for p in range(halves):
        for step, d in enumerate((3, 0, 1, 2, 4, 5, 6)):
            s = d - 3
            shifted = []
            for lev in range(levels):
                v = main[lev, p, :, rows, :]
                if s > 0:
                    v = pltpu.roll(jnp.where(lane < s, wrap[lev, p], v), LANES - s, 2)
                elif s < 0:
                    v = pltpu.roll(jnp.where(lane >= LANES + s, wrap[lev, p], v), -s, 2)
                shifted.append(v)
            sums = tap_sum(lambda lev, b: shifted[lev][b : b + width], wb, group, d, levels, width)
            for lev in range(levels):
                if step == 0:
                    total[lev, p, :, rows, :] = sums[lev]
                else:
                    total[lev, p, :, rows, :] += sums[lev]


def spread_taps(k_ref, stack, turned, wb):
    ch = k_ref.shape[3]
    for a in range(3):
        for b in range(7):
            at = (a * 7 + b) * HALF
            stack[at : at + 7, 0:ch] = k_ref[a, b]
    for half in range(2):
        turned[half] = jnp.transpose(stack[half * LANES : (half + 1) * LANES, :])

    def body(group, carry):
        rows = pl.ds(pl.multiple_of(group * HALF, HALF), HALF)
        taps = [turned[half, rows, :] for half in range(2)]
        for tap in range(TAPS):
            half, at = divmod(tap // 7 * HALF + tap % 7, LANES)
            wb[group, tap] = jnp.broadcast_to(taps[half][:, at : at + 1], (HALF, LANES))
        return carry

    lax.fori_loop(0, wb.shape[0], body, 0)


def gelu(v):
    scale = (2.0 / jnp.pi) ** 0.5
    half = 0.5 * v
    return half + half * jnp.tanh(v * (scale + (scale * 0.044715) * (v * v)))


def mlp(mine, other, resid, gain, up, down):
    values = jnp.concatenate([mine, other], axis=0).astype(F32)
    center = jnp.mean(values, axis=0, keepdims=True)
    moved = values - center
    spread = jnp.mean(moved * moved, axis=0, keepdims=True)
    normed = (moved * lax.rsqrt(spread + 1e-06) * gain).astype(BF16)
    hidden = gelu(jnp.dot(up, normed, preferred_element_type=F32)).astype(BF16)
    update = jnp.dot(down, hidden, preferred_element_type=F32)
    return resid.astype(F32) + update.astype(BF16).astype(F32)


def step_kernel(
    bands,
    state_ref,
    mask_ref,
    air_ref,
    temp_ref,
    flux_ref,
    ok_ref,
    ak_ref,
    ogain_ref,
    again_ref,
    fweight_ref,
    tweight_ref,
    oupraw_ref,
    odownraw_ref,
    aupraw_ref,
    adownraw_ref,
    onext_ref,
    anext_ref,
    stack,
    turned,
    cols_ref,
    oup_ref,
    odown_ref,
    aup_ref,
    otall,
    tl,
    fs,
    fl,
    es,
    er,
    ec,
    ew,
    ee,
    edge,
    ow,
    aw,
    oc,
    oo,
    ac,
    ao,
    owb,
    awb,
    omain,
    ototal,
    amain,
    awrap,
    atotal,
    send,
    recv,
    osend,
    orecv,
    asend,
    arecv,
):
    levels, band, och, lat = state_ref.shape
    alevels, halves, _, ach, part = air_ref.shape
    tiles = lat // LANES
    wide = band + 2 * RIM
    span = wide * 2 * RIM
    fields = fs.shape[0]
    last = band + RIM
    comp = lax.axis_index("comp")
    lon = lax.axis_index("lon")
    at = lax.axis_index("ch")
    count = 2 * bands
    place = comp * bands + lon
    west = lax.rem(place + count - 1, count)
    east = lax.rem(place + 1, count)
    o_west = {"comp": lax.div(west, bands), "lon": lax.rem(west, bands)}
    o_east = {"comp": lax.div(east, bands), "lon": lax.rem(east, bands)}
    a_west = {"lon": lax.rem(lon + bands - 1, bands)}
    a_east = {"lon": lax.rem(lon + 1, bands)}
    over = {"comp": 1 - comp}
    pair = {"ch": 1 - at}
    at_west = (lon == 0).astype(jnp.int32)
    at_east = (lon == bands - 1).astype(jnp.int32)

    barrier = pltpu.get_barrier_semaphore()
    for device in (over, pair, o_west, o_east, a_west, a_east):
        pl.semaphore_signal(barrier, inc=1, device_id=device, device_id_type=MESH)

    started = []

    def copy(src, dst, device):
        i = len(started)
        made = pltpu.make_async_remote_copy(
            src_ref=src,
            dst_ref=dst,
            send_sem=send.at[i],
            recv_sem=recv.at[i],
            device_id=device,
            device_id_type=MESH,
        )
        made.start()
        started.append(made)
        return made

    sea = mask_ref[...].astype(F32)
    own_temp = temp_ref[...] * sea
    for p in range(2):
        tl[comp, p] = own_temp[:, p * part : (p + 1) * part]
    for k in range(fields):
        low, high = flux_ref[k, :, 0, :], flux_ref[k, :, 1, :]
        fs[k] = jnp.where(comp == 0, high, low)
        fl[comp, k] = jnp.where(comp == 0, low, high)
    lane = lax.broadcasted_iota(jnp.int32, (ach, LANES), 1)

    def pack(tile, into, h, j, owner):
        base = (h * wide + RIM + j) * 2 * RIM
        begin = base + RIM * owner
        here = (lane >= begin) & (lane < begin + RIM)
        return jnp.where(here, pltpu.roll(tile, base + RIM, 1), into)

    for lev in range(1, levels):
        for j in range(band):
            v = state_ref[lev, j].astype(F32) * sea[j : j + 1, :]
            ow[lev, RIM + j] = v.astype(BF16)

    pl.semaphore_wait(barrier, 6)
    got_temp = copy(tl.at[comp], tl.at[comp], over)
    got_flux = copy(fs, fl.at[comp], over)
    deep = pl.ds(1, levels - 1)
    top = pl.ds(0, 1)
    first, final = pl.ds(RIM, RIM), pl.ds(last - RIM, RIM)
    low_rim, high_rim = pl.ds(0, RIM), pl.ds(last, RIM)
    ocean_rims = [
        copy(ow.at[deep, first], ow.at[deep, high_rim], o_west),
        copy(ow.at[deep, final], ow.at[deep, low_rim], o_east),
    ]

    for lev in range(alevels):
        packed = jnp.zeros((ach, LANES), F32)
        for h in range(halves):
            for j in range(band):
                packed = pack(air_ref[lev, h, j].astype(F32), packed, h, j, comp)
        es[lev] = packed.astype(BF16)
    got_edge = copy(es, er, over)

    stack[...] = jnp.zeros_like(stack)
    for at_row, ref in ((0, ogain_ref), (1, again_ref), (2, tweight_ref), (3, fweight_ref)):
        size = ref.shape[1]
        for begin in range(0, size, LANES):
            stop = min(begin + LANES, size)
            below = at_row + begin // LANES * HALF
            stack[below : below + ref.shape[0], 0 : stop - begin] = ref[:, begin:stop]
    flipped = jnp.transpose(stack[0:LANES, :])
    for block in range(cols_ref.shape[0] // LANES):
        cols_ref[block * LANES : (block + 1) * LANES, :] = flipped[
            :, block * HALF : (block + 1) * HALF
        ]
    spread_taps(ok_ref, stack, turned, owb)

    got_flux.wait_recv()
    for j in range(band):
        for p in range(tiles):
            inject = jnp.zeros((och, LANES), F32)
            for k in range(fields):
                inject += cols_ref[0:och, 3 + k : 4 + k] * fl[p, k, j : j + 1, :]
            cells = slice(p * LANES, (p + 1) * LANES)
            v = (state_ref[0, j, :, cells].astype(F32) + inject) * sea[j : j + 1, cells]
            ow[0, RIM + j, :, cells] = v.astype(BF16)
    ocean_rims.append(copy(ow.at[top, first], ow.at[top, high_rim], o_west))
    ocean_rims.append(copy(ow.at[top, final], ow.at[top, low_rim], o_east))

    got_temp.wait_recv()
    weight = cols_ref[0:ach, 2:3]
    for h in range(halves):
        for j in range(band):
            heat = weight * tl[h, comp, j : j + 1, :]
            aw[0, h, RIM + j] = (air_ref[0, h, j].astype(F32) + heat).astype(BF16)
            for lev in range(1, alevels):
                aw[lev, h, RIM + j] = air_ref[lev, h, j]
    air_rims = []
    every = pl.ds(0, alevels)
    for h in range(halves):
        to_west = lax.rem(h + (halves - 1) * at_west, halves)
        to_east = lax.rem(h + at_east, halves)
        air_rims.append(copy(aw.at[every, h, first], aw.at[every, to_west, high_rim], a_west))
        air_rims.append(copy(aw.at[every, h, final], aw.at[every, to_east, low_rim], a_east))
    got_edge.wait_recv()
    beyond = jnp.zeros((ach, LANES), F32)
    for h in range(halves):
        for j in range(band):
            row = jnp.broadcast_to(tl[h, 1 - comp, j : j + 1, :], (ach, LANES))
            beyond = pack(row, beyond, h, j, 1 - comp)
    ec[0] = (er[0].astype(F32) + weight * beyond).astype(BF16)
    for lev in range(1, alevels):
        ec[lev] = er[lev]
    edge_rims = [copy(ec, ee, a_west), copy(ec, ew, a_east)]

    spread_taps(ak_ref, stack, turned, awb)

    def swapped(ref):
        half = ref.shape[0] // 2
        mine = ref[pl.ds(pl.multiple_of(at * half, ROWS), half), :]
        other = ref[pl.ds(pl.multiple_of((1 - at) * half, ROWS), half), :]
        return jnp.concatenate([mine.astype(F32), other.astype(F32)], axis=0)

    oup_ref[...] = jnp.transpose(swapped(oupraw_ref)).astype(BF16)
    aup_ref[...] = jnp.transpose(swapped(aupraw_ref)).astype(BF16)
    otall[...] = jnp.transpose(odownraw_ref[...].astype(F32))
    odown_ref[...] = otall[pl.ds(pl.multiple_of(at * och, ROWS), och), :].astype(BF16)

    for made in ocean_rims:
        made.wait_recv()

    def ocean_copy(g):
        rows = pl.ds(pl.multiple_of(g * ROWS, ROWS), ROWS)
        return pltpu.make_async_remote_copy(
            src_ref=oc.at[:, :, rows, :],
            dst_ref=oo.at[:, :, rows, :],
            send_sem=osend.at[g],
            recv_sem=orecv.at[g],
            device_id=pair,
            device_id_type=MESH,
        )

    def ocean_body(g, carry):
        wider = pl.ds(pl.multiple_of(g * ROWS, ROWS), ROWS)
        for lev in range(levels):
            for p in range(tiles):
                cells = slice(p * LANES, (p + 1) * LANES)
                omain[lev, p] = ow[lev, :, wider, cells].astype(F32)

        def inner(sub, carry):
            rows = pl.ds(pl.multiple_of(sub * HALF, HALF), HALF)
            group = g * (ROWS // HALF) + sub
            ocean_group(omain, owb, ototal, rows, group, levels, tiles, band)
            return carry

        lax.fori_loop(0, ROWS // HALF, inner, 0)
        for lev in range(levels):
            for p in range(tiles):
                cells = slice(p * LANES, (p + 1) * LANES)
                oc[lev, :, wider, cells] = ototal[lev, p].astype(BF16)
        ocean_copy(g).start()
        return carry

    lax.fori_loop(0, och // ROWS, ocean_body, 0)

    for made in air_rims + edge_rims:
        made.wait_recv()
    step = band * 2 * RIM
    for lev in range(alevels):
        from_west, from_east = ew[lev].astype(F32), ee[lev].astype(F32)
        whole = ec[lev].astype(F32)
        for h in range(halves):
            west_h = lax.rem(h + (halves - 1) * at_west, halves)
            east_h = lax.rem(h + at_east, halves)
            shift = lax.rem((h - west_h) * span - step + 2 * LANES, LANES)
            here = (lane >= h * span) & (lane < h * span + 2 * RIM * RIM)
            whole = jnp.where(here, pltpu.roll(from_west, shift, 1), whole)
            shift = lax.rem((h - east_h) * span + step + 2 * LANES, LANES)
            here = (lane >= (h + 1) * span - 2 * RIM * RIM) & (lane < (h + 1) * span)
            whole = jnp.where(here, pltpu.roll(from_east, shift, 1), whole)
        edge[lev] = whole

    def air_copy(g):
        rows = pl.ds(pl.multiple_of(g * ROWS, ROWS), ROWS)
        return pltpu.make_async_remote_copy(
            src_ref=ac.at[:, :, :, rows, :],
            dst_ref=ao.at[:, :, :, rows, :],
            send_sem=asend.at[g],
            recv_sem=arecv.at[g],
            device_id=pair,
            device_id_type=MESH,
        )

    def air_body(g, carry):
        wider = pl.ds(pl.multiple_of(g * ROWS, ROWS), ROWS)
        for lev in range(alevels):
            for p in range(halves):
                amain[lev, p] = aw[lev, p, :, wider, :].astype(F32)

        def inner(sub, carry):
            rows = pl.ds(pl.multiple_of(sub * HALF, HALF), HALF)
            group = g * (ROWS // HALF) + sub
            these = pl.ds(pl.multiple_of(group * HALF, HALF), HALF)
            for lev in range(alevels):
                e = edge[lev, these, :]
                for p in range(halves):
                    for m in range(wide):
                        awrap[lev, p, m] = pltpu.roll(e, LANES - (p * wide + m) * 2 * RIM - RIM, 1)
            air_group(amain, awrap, awb, atotal, rows, group, alevels, halves, band)
            return carry

        lax.fori_loop(0, ROWS // HALF, inner, 0)
        for lev in range(alevels):
            for p in range(halves):
                ac[lev, p, :, wider, :] = atotal[lev, p].astype(BF16)
        air_copy(g).start()
        return carry

    lax.fori_loop(0, ach // ROWS, air_body, 0)

    def flat(cells):
        return jnp.concatenate([cells[j] for j in range(band)], axis=1)

    def ordered(column, ch):
        mine = cols_ref[pl.ds(pl.multiple_of(at * ch, HALF), ch), column : column + 1]
        other = cols_ref[pl.ds(pl.multiple_of((1 - at) * ch, HALF), ch), column : column + 1]
        return jnp.concatenate([mine, other], axis=0)

    lax.fori_loop(0, och // ROWS, lambda g, c: (ocean_copy(g).wait(), c)[1], 0)
    gain = ordered(0, och)

    def ocean_mlp(lev, carry):
        resid = flat(ow[lev, RIM : RIM + band])
        out = mlp(flat(oc[lev]), flat(oo[lev]), resid, gain, oup_ref[...], odown_ref[...])
        for j in range(band):
            v = out[:, j * lat : (j + 1) * lat] * mask_ref[j : j + 1, :].astype(F32)
            onext_ref[lev, j] = v.astype(BF16)
        return carry

    lax.fori_loop(0, levels, ocean_mlp, 0)
    lax.fori_loop(0, ach // ROWS, lambda g, c: (air_copy(g).wait(), c)[1], 0)
    again = ordered(1, ach)
    adown = adownraw_ref[pl.ds(pl.multiple_of(at * ach, ROWS), ach), :]

    def air_mlp(i, carry):
        lev, h = lax.div(i, halves), lax.rem(i, halves)
        resid = flat(aw[lev, h, RIM : RIM + band])
        out = mlp(flat(ac[lev, h]), flat(ao[lev, h]), resid, again, aup_ref[...], adown)
        for j in range(band):
            anext_ref[lev, h, j] = out[:, j * part : (j + 1) * part].astype(BF16)
        return carry

    lax.fori_loop(0, alevels * halves, air_mlp, 0)
    for made in started:
        made.wait_send()


def per_device(
    ocean_state,
    ocean_mask,
    air_state,
    surface_temp,
    air_fluxes,
    ocean_kernel,
    ocean_gain,
    ocean_up,
    ocean_down,
    air_kernel,
    air_gain,
    air_up,
    air_down,
    flux_weight,
    temp_weight,
):
    bands = lax.axis_size("lon")
    state = jnp.transpose(ocean_state, (0, 2, 1, 3))
    air = jnp.transpose(air_state, (0, 3, 2, 1, 4))
    levels, band, och, lat = state.shape
    alevels, halves, _, ach, part = air.shape
    fields = air_fluxes.shape[0]
    wide = band + 2 * RIM
    tiles = lat // LANES
    height = -(-max(ocean_gain.shape[0], air_gain.shape[0]) // LANES) * LANES
    ohid, ahid = ocean_up.shape[1], air_up.shape[1]
    edge = (alevels, ach, LANES)
    scratch = [
        pltpu.VMEM((2 * LANES, LANES), F32),
        pltpu.VMEM((2, LANES, LANES), F32),
        pltpu.VMEM((height, HALF), F32),
        pltpu.VMEM((ohid, 2 * och), BF16),
        pltpu.VMEM((och, ohid), BF16),
        pltpu.VMEM((ahid, 2 * ach), BF16),
        pltpu.VMEM((2 * och, ohid), F32),
        pltpu.VMEM((halves, 2, band, part), F32),
        pltpu.VMEM((fields, band, part), F32),
        pltpu.VMEM((2, fields, band, part), F32),
        pltpu.VMEM(edge, BF16),
        pltpu.VMEM(edge, BF16),
        pltpu.VMEM(edge, BF16),
        pltpu.VMEM(edge, BF16),
        pltpu.VMEM(edge, BF16),
        pltpu.VMEM(edge, F32),
        pltpu.VMEM((levels, wide, och, lat), BF16),
        pltpu.VMEM((alevels, halves, wide, ach, part), BF16),
        pltpu.VMEM(state.shape, BF16),
        pltpu.VMEM(state.shape, BF16),
        pltpu.VMEM(air.shape, BF16),
        pltpu.VMEM(air.shape, BF16),
        pltpu.VMEM((och // HALF, TAPS, HALF, LANES), F32),
        pltpu.VMEM((ach // HALF, TAPS, HALF, LANES), F32),
        pltpu.VMEM((levels, tiles, wide, ROWS, LANES), F32),
        pltpu.VMEM((levels, tiles, band, ROWS, LANES), F32),
        pltpu.VMEM((alevels, halves, wide, ROWS, LANES), F32),
        pltpu.VMEM((alevels, halves, wide, HALF, LANES), F32),
        pltpu.VMEM((alevels, halves, band, ROWS, LANES), F32),
        pltpu.SemaphoreType.DMA((9 + 2 * halves,)),
        pltpu.SemaphoreType.DMA((9 + 2 * halves,)),
        pltpu.SemaphoreType.DMA((och // ROWS,)),
        pltpu.SemaphoreType.DMA((och // ROWS,)),
        pltpu.SemaphoreType.DMA((ach // ROWS,)),
        pltpu.SemaphoreType.DMA((ach // ROWS,)),
    ]
    vmem = pl.BlockSpec(memory_space=pltpu.VMEM)
    ocean_next, air_next = pl.pallas_call(
        functools.partial(step_kernel, bands),
        out_shape=(
            jax.ShapeDtypeStruct(state.shape, BF16),
            jax.ShapeDtypeStruct(air.shape, BF16),
        ),
        in_specs=[vmem] * 15,
        out_specs=(vmem, vmem),
        scratch_shapes=scratch,
        compiler_params=pltpu.CompilerParams(
            collective_id=0, has_side_effects=True, vmem_limit_bytes=52 * 1024 * 1024
        ),
        cost_estimate=pl.CostEstimate(
            flops=2_000_000_000, bytes_accessed=4_000_000, transcendentals=3_000_000
        ),
    )(
        state,
        ocean_mask,
        air,
        surface_temp,
        air_fluxes,
        jnp.transpose(ocean_kernel, (1, 2, 3, 0)),
        jnp.transpose(air_kernel, (1, 2, 3, 0)),
        ocean_gain[None],
        air_gain[None],
        flux_weight,
        temp_weight[None],
        ocean_up,
        ocean_down,
        air_up,
        air_down.T,
    )
    return jnp.transpose(ocean_next, (0, 2, 1, 3)), jnp.transpose(air_next, (0, 3, 2, 1, 4))


def solution(mesh):
    in_specs = (
        P(None, "ch", ("comp", "lon"), None),
        P(("comp", "lon"), None),
        P(None, "ch", "lon", None, "comp"),
        P(("comp", "lon"), None),
        P(None, "lon", None, "comp"),
        P("ch", None, None, None),
        P(),
        P(),
        P(),
        P("ch", None, None, None),
        P(),
        P(),
        P(),
        P(None, "ch"),
        P("ch"),
    )
    out_specs = (P(None, "ch", ("comp", "lon"), None), P(None, "ch", "lon", None, "comp"))
    return jax.shard_map(
        per_device, mesh=mesh, in_specs=in_specs, out_specs=out_specs, check_vma=False
    )
```

```python
import functools

import jax
import jax.numpy as jnp
from jax import lax
from jax.experimental import pallas as pl
from jax.experimental.pallas import tpu as pltpu
from jax.sharding import PartitionSpec as P

LANES = 128
ROWS = 16
HALF = 8
RIM = 3
TAPS = 147
MESH = pl.DeviceIdType.MESH
F32, BF16 = jnp.float32, jnp.bfloat16


def tap_sum(values, wb, group, d, levels, width):
    sums = [None] * levels
    for a in range(3):
        for b in range(7):
            w = wb[group, a * 49 + b * 7 + d][None]
            for lev in range(levels):
                src = lev + a - 1
                if 0 <= src < levels:
                    term = w * values(src, b)
                    sums[lev] = term if sums[lev] is None else sums[lev] + term
    return sums


def ocean_group(main, wb, total, rows, group, levels, tiles, width):
    lane = lax.broadcasted_iota(jnp.int32, (width, HALF, LANES), 2)
    zero = jnp.zeros((width, HALF, LANES), F32)
    for step, d in enumerate((3, 0, 1, 2, 4, 5, 6)):
        s = d - 3
        sums = [
            tap_sum(lambda lev, b: main[lev, p, b : b + width, rows, :], wb, group, d, levels, width)
            for p in range(tiles)
        ]
        for p in range(tiles):
            for lev in range(levels):
                v = sums[p][lev]
                if s > 0:
                    beside = sums[p + 1][lev] if p + 1 < tiles else zero
                    v = pltpu.roll(jnp.where(lane < s, beside, v), LANES - s, 2)
                elif s < 0:
                    beside = sums[p - 1][lev] if p > 0 else zero
                    v = pltpu.roll(jnp.where(lane >= LANES + s, beside, v), -s, 2)
                if step == 0:
                    total[lev, p, :, rows, :] = v
                else:
                    total[lev, p, :, rows, :] += v


def air_group(main, edge, slot, wb, total, rows, group, levels, halves, width):
    lane = lax.broadcasted_iota(jnp.int32, (width, HALF, LANES), 2)
    pair = 2 * RIM
    turned = [
        [pltpu.roll(e, LANES - pair * b, 2) if b else e for b in range(7)] for e in edge
    ]
    rim = [jnp.zeros((1, HALF, LANES), F32) for _ in range(levels)]
    for d in (0, 1, 2, 4, 5, 6):
        sums = tap_sum(lambda lev, b: turned[lev][b], wb, group, d, levels, 1)
        if d < RIM:
            move, here = LANES - d, (slot >= RIM) & (slot < pair - d)
        else:
            move, here = 6 - d, (slot < RIM) & (slot >= 6 - d)
        for lev in range(levels):
            v = pltpu.roll(sums[lev], move, 2) if move % LANES else sums[lev]
            rim[lev] += jnp.where(here, v, 0.0)
    ends = (lane < RIM) | (lane >= LANES - RIM)
    for p in range(halves):
        for step, d in enumerate((3, 0, 1, 2, 4, 5, 6)):
            s = d - 3
            sums = tap_sum(
                lambda lev, b: main[lev, p, b : b + width, rows, :], wb, group, d, levels, width
            )
            for lev in range(levels):
                v = sums[lev]
                if s > 0:
                    v = pltpu.roll(jnp.where(lane < s, 0.0, v), LANES - s, 2)
                elif s < 0:
                    v = pltpu.roll(jnp.where(lane >= LANES + s, 0.0, v), -s, 2)
                if step == 0:
                    begin = p * (width + pair) * pair + RIM
                    tips = [
                        pltpu.roll(rim[lev], LANES - begin - j * pair, 2) for j in range(width)
                    ]
                    v += jnp.where(ends, jnp.concatenate(tips, axis=0), 0.0)
                    total[lev, p, :, rows, :] = v
                else:
                    total[lev, p, :, rows, :] += v


def spread_taps(k_ref, stack, turned, wb):
    ch = k_ref.shape[3]
    for a in range(3):
        for b in range(7):
            at = (a * 7 + b) * HALF
            stack[at : at + 7, 0:ch] = k_ref[a, b]
    for half in range(2):
        turned[half] = jnp.transpose(stack[half * LANES : (half + 1) * LANES, :])

    def body(group, carry):
        rows = pl.ds(pl.multiple_of(group * HALF, HALF), HALF)
        taps = [turned[half, rows, :] for half in range(2)]
        for tap in range(TAPS):
            half, at = divmod(tap // 7 * HALF + tap % 7, LANES)
            wb[group, tap] = jnp.broadcast_to(taps[half][:, at : at + 1], (HALF, LANES))
        return carry

    lax.fori_loop(0, wb.shape[0], body, 0)


def gelu(v):
    scale = (2.0 / jnp.pi) ** 0.5
    half = 0.5 * v
    return half + half * jnp.tanh(v * (scale + (scale * 0.044715) * (v * v)))


def mlp(mine, other, resid, gain, up, down):
    values = jnp.concatenate([mine, other], axis=0).astype(F32)
    center = jnp.mean(values, axis=0, keepdims=True)
    moved = values - center
    spread = jnp.mean(moved * moved, axis=0, keepdims=True)
    normed = (moved * lax.rsqrt(spread + 1e-06) * gain).astype(BF16)
    hidden = gelu(jnp.dot(up, normed, preferred_element_type=F32)).astype(BF16)
    update = jnp.dot(down, hidden, preferred_element_type=F32)
    return resid.astype(F32) + update.astype(BF16).astype(F32)


def step_kernel(
    bands,
    state_ref,
    mask_ref,
    air_ref,
    temp_ref,
    flux_ref,
    ok_ref,
    ak_ref,
    ogain_ref,
    again_ref,
    fweight_ref,
    tweight_ref,
    oupraw_ref,
    odownraw_ref,
    aupraw_ref,
    adownraw_ref,
    onext_ref,
    anext_ref,
    stack,
    turned,
    cols_ref,
    oup_ref,
    odown_ref,
    aup_ref,
    otall,
    tl,
    fs,
    fl,
    es,
    er,
    ec,
    ew,
    ee,
    edge,
    ow,
    aw,
    oc,
    oo,
    ac,
    ao,
    owb,
    awb,
    omain,
    ototal,
    amain,
    slot_ref,
    atotal,
    send,
    recv,
    osend,
    orecv,
    asend,
    arecv,
):
    levels, band, och, lat = state_ref.shape
    alevels, halves, _, ach, part = air_ref.shape
    tiles = lat // LANES
    wide = band + 2 * RIM
    span = wide * 2 * RIM
    fields = fs.shape[0]
    last = band + RIM
    comp = lax.axis_index("comp")
    lon = lax.axis_index("lon")
    at = lax.axis_index("ch")
    count = 2 * bands
    place = comp * bands + lon
    west = lax.rem(place + count - 1, count)
    east = lax.rem(place + 1, count)
    o_west = {"comp": lax.div(west, bands), "lon": lax.rem(west, bands)}
    o_east = {"comp": lax.div(east, bands), "lon": lax.rem(east, bands)}
    a_west = {"lon": lax.rem(lon + bands - 1, bands)}
    a_east = {"lon": lax.rem(lon + 1, bands)}
    over = {"comp": 1 - comp}
    pair = {"ch": 1 - at}
    at_west = (lon == 0).astype(jnp.int32)
    at_east = (lon == bands - 1).astype(jnp.int32)

    barrier = pltpu.get_barrier_semaphore()
    for device in (over, pair, o_west, o_east, a_west, a_east):
        pl.semaphore_signal(barrier, inc=1, device_id=device, device_id_type=MESH)

    started = []

    def copy(src, dst, device):
        i = len(started)
        made = pltpu.make_async_remote_copy(
            src_ref=src,
            dst_ref=dst,
            send_sem=send.at[i],
            recv_sem=recv.at[i],
            device_id=device,
            device_id_type=MESH,
        )
        made.start()
        started.append(made)
        return made

    sea = mask_ref[...].astype(F32)
    own_temp = temp_ref[...] * sea
    for p in range(2):
        tl[comp, p] = own_temp[:, p * part : (p + 1) * part]
    for k in range(fields):
        low, high = flux_ref[k, :, 0, :], flux_ref[k, :, 1, :]
        fs[k] = jnp.where(comp == 0, high, low)
        fl[comp, k] = jnp.where(comp == 0, low, high)
    lane = lax.broadcasted_iota(jnp.int32, (ach, LANES), 1)

    def pack(tile, into, h, j, owner):
        base = (h * wide + RIM + j) * 2 * RIM
        begin = base + RIM * (1 - owner)
        here = (lane >= begin) & (lane < begin + RIM)
        return jnp.where(here, pltpu.roll(tile, base + 2 * RIM * (1 - owner), 1), into)

    for lev in range(1, levels):
        for j in range(band):
            v = state_ref[lev, j].astype(F32) * sea[j : j + 1, :]
            ow[lev, RIM + j] = v.astype(BF16)

    pl.semaphore_wait(barrier, 6)
    got_temp = copy(tl.at[comp], tl.at[comp], over)
    got_flux = copy(fs, fl.at[comp], over)
    deep = pl.ds(1, levels - 1)
    top = pl.ds(0, 1)
    first, final = pl.ds(RIM, RIM), pl.ds(last - RIM, RIM)
    low_rim, high_rim = pl.ds(0, RIM), pl.ds(last, RIM)
    ocean_rims = [
        copy(ow.at[deep, first], ow.at[deep, high_rim], o_west),
        copy(ow.at[deep, final], ow.at[deep, low_rim], o_east),
    ]

    for lev in range(alevels):
        packed = jnp.zeros((ach, LANES), F32)
        for h in range(halves):
            for j in range(band):
                packed = pack(air_ref[lev, h, j].astype(F32), packed, h, j, comp)
        es[lev] = packed.astype(BF16)
    got_edge = copy(es, er, over)

    stack[...] = jnp.zeros_like(stack)
    for at_row, ref in ((0, ogain_ref), (1, again_ref), (2, tweight_ref), (3, fweight_ref)):
        size = ref.shape[1]
        for begin in range(0, size, LANES):
            stop = min(begin + LANES, size)
            below = at_row + begin // LANES * HALF
            stack[below : below + ref.shape[0], 0 : stop - begin] = ref[:, begin:stop]
    flipped = jnp.transpose(stack[0:LANES, :])
    for block in range(cols_ref.shape[0] // LANES):
        cols_ref[block * LANES : (block + 1) * LANES, :] = flipped[
            :, block * HALF : (block + 1) * HALF
        ]
    spread_taps(ok_ref, stack, turned, owb)

    got_flux.wait_recv()
    for j in range(band):
        for p in range(tiles):
            inject = jnp.zeros((och, LANES), F32)
            for k in range(fields):
                inject += cols_ref[0:och, 3 + k : 4 + k] * fl[p, k, j : j + 1, :]
            cells = slice(p * LANES, (p + 1) * LANES)
            v = (state_ref[0, j, :, cells].astype(F32) + inject) * sea[j : j + 1, cells]
            ow[0, RIM + j, :, cells] = v.astype(BF16)
    ocean_rims.append(copy(ow.at[top, first], ow.at[top, high_rim], o_west))
    ocean_rims.append(copy(ow.at[top, final], ow.at[top, low_rim], o_east))

    got_temp.wait_recv()
    weight = cols_ref[0:ach, 2:3]
    for h in range(halves):
        for j in range(band):
            heat = weight * tl[h, comp, j : j + 1, :]
            aw[0, h, RIM + j] = (air_ref[0, h, j].astype(F32) + heat).astype(BF16)
            for lev in range(1, alevels):
                aw[lev, h, RIM + j] = air_ref[lev, h, j]
    got_edge.wait_recv()
    beyond = jnp.zeros((ach, LANES), F32)
    for h in range(halves):
        for j in range(band):
            row = jnp.broadcast_to(tl[h, 1 - comp, j : j + 1, :], (ach, LANES))
            beyond = pack(row, beyond, h, j, 1 - comp)
    ec[0] = (er[0].astype(F32) + weight * beyond).astype(BF16)
    for lev in range(1, alevels):
        ec[lev] = er[lev]

    spread_taps(ak_ref, stack, turned, awb)

    def swapped(ref):
        half = ref.shape[0] // 2
        mine = ref[pl.ds(pl.multiple_of(at * half, ROWS), half), :]
        other = ref[pl.ds(pl.multiple_of((1 - at) * half, ROWS), half), :]
        return jnp.concatenate([mine.astype(F32), other.astype(F32)], axis=0)

    oup_ref[...] = jnp.transpose(swapped(oupraw_ref)).astype(BF16)
    aup_ref[...] = jnp.transpose(swapped(aupraw_ref)).astype(BF16)
    otall[...] = jnp.transpose(odownraw_ref[...].astype(F32))
    odown_ref[...] = otall[pl.ds(pl.multiple_of(at * och, ROWS), och), :].astype(BF16)

    slot_ref[...] = lax.rem(
        lax.broadcasted_iota(jnp.int32, (1, HALF, LANES), 2), jnp.int32(2 * RIM)
    )
    for made in ocean_rims:
        made.wait_recv()
    edge_rims = [copy(ec, ee, a_west), copy(ec, ew, a_east)]
    air_rims = []
    every = pl.ds(0, alevels)
    for h in range(halves):
        to_west = lax.rem(h + (halves - 1) * at_west, halves)
        to_east = lax.rem(h + at_east, halves)
        air_rims.append(copy(aw.at[every, h, first], aw.at[every, to_west, high_rim], a_west))
        air_rims.append(copy(aw.at[every, h, final], aw.at[every, to_east, low_rim], a_east))

    def ocean_copy(g):
        rows = pl.ds(pl.multiple_of(g * ROWS, ROWS), ROWS)
        return pltpu.make_async_remote_copy(
            src_ref=oc.at[:, :, rows, :],
            dst_ref=oo.at[:, :, rows, :],
            send_sem=osend.at[g],
            recv_sem=orecv.at[g],
            device_id=pair,
            device_id_type=MESH,
        )

    def ocean_body(g, carry):
        wider = pl.ds(pl.multiple_of(g * ROWS, ROWS), ROWS)
        for lev in range(levels):
            for p in range(tiles):
                cells = slice(p * LANES, (p + 1) * LANES)
                omain[lev, p] = ow[lev, :, wider, cells].astype(F32)

        def inner(sub, carry):
            rows = pl.ds(pl.multiple_of(sub * HALF, HALF), HALF)
            group = g * (ROWS // HALF) + sub
            ocean_group(omain, owb, ototal, rows, group, levels, tiles, band)
            return carry

        lax.fori_loop(0, ROWS // HALF, inner, 0)
        for lev in range(levels):
            for p in range(tiles):
                cells = slice(p * LANES, (p + 1) * LANES)
                oc[lev, :, wider, cells] = ototal[lev, p].astype(BF16)
        ocean_copy(g).start()
        return carry

    lax.fori_loop(0, och // ROWS, ocean_body, 0)

    for made in air_rims + edge_rims:
        made.wait_recv()
    step = band * 2 * RIM
    for lev in range(alevels):
        from_west, from_east = ew[lev].astype(F32), ee[lev].astype(F32)
        whole = ec[lev].astype(F32)
        for h in range(halves):
            west_h = lax.rem(h + (halves - 1) * at_west, halves)
            east_h = lax.rem(h + at_east, halves)
            shift = lax.rem((h - west_h) * span - step + 2 * LANES, LANES)
            here = (lane >= h * span) & (lane < h * span + 2 * RIM * RIM)
            whole = jnp.where(here, pltpu.roll(from_west, shift, 1), whole)
            shift = lax.rem((h - east_h) * span + step + 2 * LANES, LANES)
            here = (lane >= (h + 1) * span - 2 * RIM * RIM) & (lane < (h + 1) * span)
            whole = jnp.where(here, pltpu.roll(from_east, shift, 1), whole)
        edge[lev] = whole

    def air_copy(g):
        rows = pl.ds(pl.multiple_of(g * ROWS, ROWS), ROWS)
        return pltpu.make_async_remote_copy(
            src_ref=ac.at[:, :, :, rows, :],
            dst_ref=ao.at[:, :, :, rows, :],
            send_sem=asend.at[g],
            recv_sem=arecv.at[g],
            device_id=pair,
            device_id_type=MESH,
        )

    def air_body(g, carry):
        wider = pl.ds(pl.multiple_of(g * ROWS, ROWS), ROWS)
        for lev in range(alevels):
            for p in range(halves):
                amain[lev, p] = aw[lev, p, :, wider, :].astype(F32)

        def inner(sub, carry):
            rows = pl.ds(pl.multiple_of(sub * HALF, HALF), HALF)
            group = g * (ROWS // HALF) + sub
            these = pl.ds(pl.multiple_of(group * HALF, HALF), HALF)
            ends = [edge[lev, these, :][None] for lev in range(alevels)]
            air_group(amain, ends, slot_ref[...], awb, atotal, rows, group, alevels, halves, band)
            return carry

        lax.fori_loop(0, ROWS // HALF, inner, 0)
        for lev in range(alevels):
            for p in range(halves):
                ac[lev, p, :, wider, :] = atotal[lev, p].astype(BF16)
        air_copy(g).start()
        return carry

    lax.fori_loop(0, ach // ROWS, air_body, 0)

    def flat(cells):
        return jnp.concatenate([cells[j] for j in range(band)], axis=1)

    def ordered(column, ch):
        mine = cols_ref[pl.ds(pl.multiple_of(at * ch, HALF), ch), column : column + 1]
        other = cols_ref[pl.ds(pl.multiple_of((1 - at) * ch, HALF), ch), column : column + 1]
        return jnp.concatenate([mine, other], axis=0)

    lax.fori_loop(0, och // ROWS, lambda g, c: (ocean_copy(g).wait(), c)[1], 0)
    gain = ordered(0, och)

    def ocean_mlp(lev, carry):
        resid = flat(ow[lev, RIM : RIM + band])
        out = mlp(flat(oc[lev]), flat(oo[lev]), resid, gain, oup_ref[...], odown_ref[...])
        for j in range(band):
            v = out[:, j * lat : (j + 1) * lat] * mask_ref[j : j + 1, :].astype(F32)
            onext_ref[lev, j] = v.astype(BF16)
        return carry

    lax.fori_loop(0, levels, ocean_mlp, 0)
    lax.fori_loop(0, ach // ROWS, lambda g, c: (air_copy(g).wait(), c)[1], 0)
    again = ordered(1, ach)
    adown = adownraw_ref[pl.ds(pl.multiple_of(at * ach, ROWS), ach), :]

    def air_mlp(i, carry):
        lev, h = lax.div(i, halves), lax.rem(i, halves)
        resid = flat(aw[lev, h, RIM : RIM + band])
        out = mlp(flat(ac[lev, h]), flat(ao[lev, h]), resid, again, aup_ref[...], adown)
        for j in range(band):
            anext_ref[lev, h, j] = out[:, j * part : (j + 1) * part].astype(BF16)
        return carry

    lax.fori_loop(0, alevels * halves, air_mlp, 0)
    for made in started:
        made.wait_send()


def per_device(
    ocean_state,
    ocean_mask,
    air_state,
    surface_temp,
    air_fluxes,
    ocean_kernel,
    ocean_gain,
    ocean_up,
    ocean_down,
    air_kernel,
    air_gain,
    air_up,
    air_down,
    flux_weight,
    temp_weight,
):
    bands = lax.axis_size("lon")
    state = jnp.transpose(ocean_state, (0, 2, 1, 3))
    air = jnp.transpose(air_state, (0, 3, 2, 1, 4))
    levels, band, och, lat = state.shape
    alevels, halves, _, ach, part = air.shape
    fields = air_fluxes.shape[0]
    wide = band + 2 * RIM
    tiles = lat // LANES
    height = -(-max(ocean_gain.shape[0], air_gain.shape[0]) // LANES) * LANES
    ohid, ahid = ocean_up.shape[1], air_up.shape[1]
    edge = (alevels, ach, LANES)
    scratch = [
        pltpu.VMEM((2 * LANES, LANES), F32),
        pltpu.VMEM((2, LANES, LANES), F32),
        pltpu.VMEM((height, HALF), F32),
        pltpu.VMEM((ohid, 2 * och), BF16),
        pltpu.VMEM((och, ohid), BF16),
        pltpu.VMEM((ahid, 2 * ach), BF16),
        pltpu.VMEM((2 * och, ohid), F32),
        pltpu.VMEM((halves, 2, band, part), F32),
        pltpu.VMEM((fields, band, part), F32),
        pltpu.VMEM((2, fields, band, part), F32),
        pltpu.VMEM(edge, BF16),
        pltpu.VMEM(edge, BF16),
        pltpu.VMEM(edge, BF16),
        pltpu.VMEM(edge, BF16),
        pltpu.VMEM(edge, BF16),
        pltpu.VMEM(edge, F32),
        pltpu.VMEM((levels, wide, och, lat), BF16),
        pltpu.VMEM((alevels, halves, wide, ach, part), BF16),
        pltpu.VMEM(state.shape, BF16),
        pltpu.VMEM(state.shape, BF16),
        pltpu.VMEM(air.shape, BF16),
        pltpu.VMEM(air.shape, BF16),
        pltpu.VMEM((och // HALF, TAPS, HALF, LANES), F32),
        pltpu.VMEM((ach // HALF, TAPS, HALF, LANES), F32),
        pltpu.VMEM((levels, tiles, wide, ROWS, LANES), F32),
        pltpu.VMEM((levels, tiles, band, ROWS, LANES), F32),
        pltpu.VMEM((alevels, halves, wide, ROWS, LANES), F32),
        pltpu.VMEM((1, HALF, LANES), jnp.int32),
        pltpu.VMEM((alevels, halves, band, ROWS, LANES), F32),
        pltpu.SemaphoreType.DMA((9 + 2 * halves,)),
        pltpu.SemaphoreType.DMA((9 + 2 * halves,)),
        pltpu.SemaphoreType.DMA((och // ROWS,)),
        pltpu.SemaphoreType.DMA((och // ROWS,)),
        pltpu.SemaphoreType.DMA((ach // ROWS,)),
        pltpu.SemaphoreType.DMA((ach // ROWS,)),
    ]
    vmem = pl.BlockSpec(memory_space=pltpu.VMEM)
    ocean_next, air_next = pl.pallas_call(
        functools.partial(step_kernel, bands),
        out_shape=(
            jax.ShapeDtypeStruct(state.shape, BF16),
            jax.ShapeDtypeStruct(air.shape, BF16),
        ),
        in_specs=[vmem] * 15,
        out_specs=(vmem, vmem),
        scratch_shapes=scratch,
        compiler_params=pltpu.CompilerParams(
            collective_id=0, has_side_effects=True, vmem_limit_bytes=52 * 1024 * 1024
        ),
        cost_estimate=pl.CostEstimate(
            flops=2_000_000_000, bytes_accessed=4_000_000, transcendentals=3_000_000
        ),
    )(
        state,
        ocean_mask,
        air,
        surface_temp,
        air_fluxes,
        jnp.transpose(ocean_kernel, (1, 2, 3, 0)),
        jnp.transpose(air_kernel, (1, 2, 3, 0)),
        ocean_gain[None],
        air_gain[None],
        flux_weight,
        temp_weight[None],
        ocean_up,
        ocean_down,
        air_up,
        air_down.T,
    )
    return jnp.transpose(ocean_next, (0, 2, 1, 3)), jnp.transpose(air_next, (0, 3, 2, 1, 4))


def solution(mesh):
    in_specs = (
        P(None, "ch", ("comp", "lon"), None),
        P(("comp", "lon"), None),
        P(None, "ch", "lon", None, "comp"),
        P(("comp", "lon"), None),
        P(None, "lon", None, "comp"),
        P("ch", None, None, None),
        P(),
        P(),
        P(),
        P("ch", None, None, None),
        P(),
        P(),
        P(),
        P(None, "ch"),
        P("ch"),
    )
    out_specs = (P(None, "ch", ("comp", "lon"), None), P(None, "ch", "lon", None, "comp"))
    return jax.shard_map(
        per_device, mesh=mesh, in_specs=in_specs, out_specs=out_specs, check_vma=False
    )
```
